256 devices in a mesh: ctx: 128 (over y, x_lo, z, core), head: 2 (over x_hi).
Axes of the slice: x: 4 (x_hi: 2, x_lo: 2; x = x_hi * 2 + x_lo), y: 4, z: 8, core: 2. Of those that a mesh axis runs over, the one named last changes fastest.
Arguments:
- q_raw: bfloat16 [32768, 4096], P('ctx', 'head'), may hold values from -8 to 8
- k_raw: bfloat16 [32768, 4096], P('ctx', 'head'), may hold values from -8 to 8
- v_raw: bfloat16 [32768, 4096], P('ctx', 'head'), may hold values from -8 to 8
- g_raw: bfloat16 [32768, 4096], P('ctx', 'head'), may hold values from -6 to 6
- short_filters: float32 [4, 3, 4096], P(None, None, 'head'), may hold values from 0.2 to 1
- long_filter: float32 [7, 4096], P(None, 'head'), may hold values from -2 to 2
- out_gain: float32 [4096], P('head'), may hold values from 0.25 to 1.75
- block_lists: int32 [256, 7], replicated, may hold values from -1 to 255, as said below
Outputs:
- normed: bfloat16 [32768, 4096], P('ctx', 'head')
The draws below stay inside these ranges and needn't reach their ends.
Inputs may be any that keep to these rules, and one draw needn't show every extreme that they name: `block_lists`: row i holds in slot t < 3 the block i - t, or -1 where i - t < 0. In slot 3 + s it holds either -1 or p + s * 64, the latter only where that is at most i - 3, with one offset p of 0 to 60 for the whole array. Each row keeps or drops each such global entry by its own drawn choice. The last row keeps all of them.
All inputs are finite; a program needn't handle non-finite values.
Results may differ from the reference program's by a relative error of at most 0.0086.
Values may be sent and summed in bfloat16 or wider, within the bound.
A program may use at most 128 MiB of HBM per device.

```python
import math
import jax
import jax.numpy as jnp
from jax import lax

D = 4096
HEADS = 32
HS = 128
BLK = 128
BAND = 3
NGLOB = 4
TAPS = 3
TAPS_LONG = 7
TOKENS = 32768
NBLK = 256
STRIDE = 64


def drawn_streams(key):
    base_key = jax.random.fold_in(key, 101)
    first_stream = jnp.clip(jax.random.normal(jax.random.fold_in(base_key, 2), (TOKENS, D), jnp.float32), -6.0, 6.0)
    second_stream = jnp.clip(jax.random.normal(jax.random.fold_in(base_key, 3), (TOKENS, D), jnp.float32), -6.0, 6.0)
    return (first_stream, second_stream)


def draw_q_raw(key, part):
    return drawn_streams(key)[0].astype(jnp.bfloat16)


def draw_k_raw(key, part):
    return drawn_streams(key)[1].astype(jnp.bfloat16)


def draw_v_raw(key, part):
    base_key = jax.random.fold_in(key, 202)
    channel_ramp = jnp.arange(D, dtype=jnp.float32)[None, :] / (D - 1) - 0.5
    normal_part = jnp.clip(jax.random.normal(base_key, (TOKENS, D), jnp.float32), -4.5, 4.5)
    values = normal_part * jnp.exp(channel_ramp * math.log(3.0))
    return values.astype(jnp.bfloat16)


def draw_block_lists(key, part):
    offset_value = jax.random.randint(jax.random.fold_in(key, 303), (), 0, STRIDE - BAND)
    keep_draw = jax.random.randint(jax.random.fold_in(key, 304), (NBLK, NGLOB), 0, 4)
    last_row = jnp.arange(NBLK, dtype=jnp.int32)[:, None] == NBLK - 1
    keep_mask = (keep_draw > 0) | last_row
    row_ids = jnp.arange(NBLK, dtype=jnp.int32)[:, None]
    band_part = row_ids - jnp.arange(BAND, dtype=jnp.int32)[None, :]
    band_part = jnp.where(band_part >= 0, band_part, -1)
    global_part = offset_value + STRIDE * jnp.arange(NGLOB, dtype=jnp.int32)[None, :]
    global_part = jnp.where((global_part <= row_ids - BAND) & keep_mask, global_part, -1)
    return jnp.concatenate([band_part, global_part], axis=1).astype(jnp.int32)


def steps_of(rng, dims, shards, smallest, top_value):
    level, own = 1.0, jax.random.fold_in(rng, 6)
    for position, parts in shards:
        steps = jnp.exp(jax.random.uniform(jax.random.fold_in(own, position), (parts,), jnp.float32, smallest / len(shards), top_value / len(shards)))
        level = level * jnp.repeat(steps, dims[position] // parts).reshape([-1 if axis == position else 1 for axis in range(len(dims))])
    return level


def scatter_about(key, shape, deviation, reach, pieces=(), kind=jnp.bfloat16):
    drawn = jax.random.normal(key, shape, jnp.float32) * deviation
    if len(pieces) > 0:
        drawn = steps_of(key, shape, pieces, -0.22, 0.18) * drawn
    return jnp.clip(drawn, min=-reach, max=reach).astype(kind)


def setup_inputs(seed: int = 0) -> dict:
    keys = jax.random.split(jax.random.key(seed), 9)
    q_raw = draw_q_raw(jax.random.fold_in(keys[8], 71), 0)
    k_raw = draw_k_raw(jax.random.fold_in(keys[8], 71), 0)
    v_raw = draw_v_raw(jax.random.fold_in(keys[8], 71), 0)
    g_raw = scatter_about(keys[3], (TOKENS, D), 1.0, 6.0, ((0, 128), (1, 2)))
    short_filters = jnp.clip(jnp.exp(math.log(1.0) - 1.609438 * jax.random.uniform(keys[4], (4, TAPS, D), jnp.float32) ** steps_of(keys[4], (4, TAPS, D), ((2, 2),), -0.2, 0.2)), 0.2, 1.0)
    long_filter = scatter_about(keys[5], (TAPS_LONG, D), TAPS_LONG ** -0.5, 2.0, ((1, 2),), jnp.float32)
    out_gain = jnp.clip(1.0 + 0.15 * jax.random.normal(keys[6], (D,), jnp.float32), 0.25, 1.75)
    block_lists = draw_block_lists(jax.random.fold_in(keys[8], 71), 0)
    return dict(q_raw=q_raw, k_raw=k_raw, v_raw=v_raw, g_raw=g_raw, short_filters=short_filters, long_filter=long_filter, out_gain=out_gain, block_lists=block_lists)


def causal_filter(signal, weights):
    tap_count = weights.shape[0]
    length = signal.shape[0]
    padded = jnp.pad(signal, ((tap_count - 1, 0), (0, 0)))
    result = jnp.zeros(signal.shape, jnp.float32)
    for offset in range(tap_count):
        begin_row = tap_count - 1 - offset
        result = result + weights[offset] * padded[begin_row:begin_row + length]
    return result

def reference(q_raw, k_raw, v_raw, g_raw, short_filters, long_filter, out_gain, block_lists):
    token_count = q_raw.shape[0]
    block_count = token_count // BLK
    safe_lists = jnp.maximum(block_lists, 0).astype(jnp.int32)
    inside = jnp.arange(BLK, dtype=jnp.int32)
    query_pos = jnp.arange(block_count, dtype=jnp.int32)[:, None] * BLK + inside[None, :]
    key_pos = safe_lists[:, :, None] * BLK + inside[None, None, :]
    allowed = (block_lists >= 0)[:, None, :, None] & (key_pos[:, None, :, :] <= query_pos[:, :, None, None])

    def one_head(head_index):
        first_col = head_index * HS

        def columns(matrix):
            return lax.dynamic_slice_in_dim(matrix, first_col, HS, 1)
        feat_q = causal_filter(columns(q_raw).astype(jnp.float32), columns(short_filters[0]))
        feat_k = causal_filter(columns(k_raw).astype(jnp.float32), columns(short_filters[1]))
        feat_v = causal_filter(columns(v_raw).astype(jnp.float32), columns(short_filters[2]))
        feat_g = causal_filter(columns(g_raw).astype(jnp.float32), columns(short_filters[3]))
        query_feat = lax.optimization_barrier(feat_q.astype(jnp.bfloat16)).astype(jnp.float32)
        key_feat = lax.optimization_barrier(feat_k.astype(jnp.bfloat16)).astype(jnp.float32)
        gated_inner = feat_g * feat_v
        filtered = causal_filter(gated_inner, columns(long_filter))
        value_feat = lax.optimization_barrier(filtered.astype(jnp.bfloat16)).astype(jnp.float32)
        query_blocks = query_feat.reshape(block_count, BLK, HS)
        key_blocks = key_feat.reshape(block_count, BLK, HS)[safe_lists]
        value_blocks = value_feat.reshape(block_count, BLK, HS)[safe_lists]
        scores = jnp.einsum('iqd,iekd->iqek', query_blocks, key_blocks) / math.sqrt(HS)
        scores = jnp.where(allowed, scores, -jnp.inf)
        highest = lax.optimization_barrier(jnp.max(scores, axis=(2, 3), keepdims=True))
        weights = jnp.exp(scores - highest)
        denominator = lax.optimization_barrier(jnp.sum(weights, axis=(2, 3)))
        rounded = lax.optimization_barrier(weights.astype(jnp.bfloat16)).astype(jnp.float32)
        blended = jnp.einsum('iqek,iekd->iqd', rounded, value_blocks) / denominator[:, :, None]
        return blended.reshape(token_count, HS)
    attended = lax.map(one_head, jnp.arange(HEADS, dtype=jnp.int32))
    energy = lax.optimization_barrier(jnp.sum(attended * attended, axis=(0, 2))) / D
    merged = jnp.transpose(attended, (1, 0, 2)).reshape(token_count, D)
    return (merged * out_gain * lax.rsqrt(energy + 1e-06)[:, None]).astype(jnp.bfloat16)
```

```python
import functools
import math

import jax
import jax.numpy as jnp
from jax import lax
from jax.experimental import pallas as pl
from jax.experimental.pallas import tpu as pltpu
from jax.sharding import PartitionSpec as P

D = 4096
HS = 128
BLK = 128
BAND = 3
NGLOB = 4
TAPS = 3
TAPS_LONG = 7
ROWS = 256
HEADS_HERE = 16
HALF = 8
HALO = 16
PART = 64
MESH = pl.DeviceIdType.MESH
F32 = jnp.float32
BF16 = jnp.bfloat16
VMEM = pltpu.VMEM
MIB = 1024 * 1024


def taps_of(ext, weights, count):
    total = weights[0:1] * ext
    for s in range(1, count):
        total = total + weights[s : s + 1] * pltpu.roll(ext, s, 0)
    return total


def features_kernel(
    parity_ref, q_ref, k_ref, v_ref, g_ref, sf_ref, lf_ref,
    qf_ref, kv_ref, cand_ref, halo, send_sem, recv_sem,
):
    me = lax.axis_index("ctx")
    last = lax.axis_size("ctx") - 1
    streams = (q_ref, k_ref, v_ref, g_ref)
    barrier = pltpu.get_barrier_semaphore()

    for other in ((me + last) % (last + 1), (me + 1) % (last + 1)):
        pl.semaphore_signal(barrier, inc=1, device_id={"ctx": other}, device_id_type=MESH)
    pl.semaphore_wait(barrier, 2)

    def tail_copy(i):
        return pltpu.make_async_remote_copy(
            src_ref=streams[i].at[pl.ds(ROWS - HALO, HALO)],
            dst_ref=halo.at[i],
            send_sem=send_sem.at[i],
            recv_sem=recv_sem.at[i],
            device_id={"ctx": me + 1},
            device_id_type=MESH,
        )

    @pl.when(me < last)
    def _():
        for i in range(4):
            tail_copy(i).start()

    @pl.when(me == 0)
    def _():
        halo[...] = jnp.zeros_like(halo)

    def part(h, r):
        cols = pl.ds(pl.multiple_of(h * HS, HS), HS)

        def extended(i):
            if r == 0:
                before = halo[i, :, cols].astype(F32)
                return jnp.concatenate([before, streams[i][0:PART, cols].astype(F32)], 0)
            return streams[i][r * PART - HALO : (r + 1) * PART, cols].astype(F32)

        feats = [taps_of(extended(i), sf_ref[i, :, cols], TAPS) for i in range(4)]
        values = taps_of(feats[3] * feats[2], lf_ref[:, cols], TAPS_LONG)
        qf_ref[h, r * PART : (r + 1) * PART, :] = feats[0][HALO:].astype(BF16)
        low = r * PART % BLK
        kv_ref[r * PART // BLK, h, 0, low : low + PART, :] = feats[1][HALO:].astype(BF16)
        kv_ref[r * PART // BLK, h, 1, low : low + PART, :] = values[HALO:].astype(BF16)

    @pl.loop(0, HEADS_HERE)
    def _(h):
        for r in range(1, ROWS // PART):
            part(h, r)

    @pl.when(me > 0)
    def _():
        for i in range(4):
            tail_copy(i).wait_recv()

    parity = parity_ref[0]

    @pl.loop(0, HEADS_HERE)
    def _(h):
        part(h, 0)
        cand_ref[h] = kv_ref[parity, h]

    @pl.when(me < last)
    def _():
        for i in range(4):
            tail_copy(i).wait_send()


def features(parity, q_raw, k_raw, v_raw, g_raw, short_filters, long_filter):
    vm = pl.BlockSpec(memory_space=VMEM)
    return pl.pallas_call(
        features_kernel,
        out_shape=(
            jax.ShapeDtypeStruct((HEADS_HERE, ROWS, HS), BF16),
            jax.ShapeDtypeStruct((2, HEADS_HERE, 2, BLK, HS), BF16),
            jax.ShapeDtypeStruct((HEADS_HERE, 2, BLK, HS), BF16),
        ),
        in_specs=[pl.BlockSpec(memory_space=pltpu.SMEM)] + [vm] * 6,
        out_specs=(vm, vm, vm),
        scratch_shapes=[
            VMEM((4, HALO, HEADS_HERE * HS), BF16),
            pltpu.SemaphoreType.DMA((4,)),
            pltpu.SemaphoreType.DMA((4,)),
        ],
        compiler_params=pltpu.CompilerParams(
            collective_id=0, has_side_effects=True, vmem_limit_bytes=32 * MIB
        ),
        name="features",
    )(parity, q_raw, k_raw, v_raw, g_raw, short_filters, long_filter)


def exchange_kernel(source, kv_ref, cand_ref, band_ref, glob_ref, send_sem, recv_sem, band_send, band_recv, fill_sem):
    x0, z0, c0 = source // 16, source // 2 % 8, source % 2
    me = lax.axis_index("ctx")
    last = lax.axis_size("ctx") - 1
    core = me % 2
    z = me // 2 % 8
    x = me // 16 % 2
    y = me // 32
    steps = (z0 - z + 8) % 8

    def at(yy, xx, zz, cc):
        return ((yy * 2 + xx) * 8 + zz) * 2 + cc

    z_up, z_down = at(y, x, (z + 1) % 8, core), at(y, x, (z + 7) % 8, core)
    x_other = at(y, 1 - x, z, core)
    y_up, y_down = at((y + 1) % 4, x, z, core), at((y + 3) % 4, x, z, core)
    sibling = at(y, x, z, 1 - core)
    outer = (me + last + 2 * core) % (last + 1)

    barrier = pltpu.get_barrier_semaphore()
    for other in (z_up, z_down, x_other, y_up, y_down, sibling, outer):
        pl.semaphore_signal(barrier, inc=1, device_id={"ctx": other}, device_id_type=MESH)
    pl.semaphore_wait(barrier, 7)

    def band_copy():
        return pltpu.make_async_remote_copy(
            src_ref=kv_ref, dst_ref=band_ref, send_sem=band_send, recv_sem=band_recv,
            device_id={"ctx": me + 1}, device_id_type=MESH,
        )

    @pl.when(me < last)
    def _():
        band_copy().start()

    @pl.when(me == 0)
    def _():
        pltpu.make_async_copy(kv_ref, band_ref, band_recv).start()

    main = x == (x0 + core) % 2
    at_source = (x == x0) & (steps == 0)
    mine, theirs = core * HALF, (1 - core) * HALF

    plans = []
    for s in range(NGLOB):
        plane = y == s
        down_z = plane & main & (steps < 7)
        over_x = plane & (
            (main & jnp.logical_not((core == 1) & (steps == 0)))
            | (jnp.logical_not(main) & (core == 1) & (steps == 0))
        )
        never = y < 0
        up = [
            (y == 0) | ((y == 1) & (core == 0)),
            (y == 1) | ((y == 2) & (core == 0)),
            y == 2,
            never,
        ][s]
        down = [
            (y == 0) | ((y == 3) & (core == 1)),
            ((y == 1) | (y == 0)) & (core == 1),
            never,
            never,
        ][s]
        needs = y >= s
        owner = plane & at_source & (core == c0)
        near_owner = plane & at_source & (core != c0)
        holds = needs if s != 1 else (needs | ((y == 0) & (core == 1)))
        share = needs & jnp.logical_not(near_owner)
        routes = []
        if s < 3:
            routes += [(2, up, y_up)]
        if s < 2:
            routes += [(3, down, y_down)]
        routes = [(0, down_z, z_down), (1, over_x, x_other)] + routes + [(4, share, sibling)]
        plans.append((needs, owner, holds, routes))

    def send(s, h, kind, target):
        return pltpu.make_async_remote_copy(
            src_ref=glob_ref.at[s, h], dst_ref=glob_ref.at[s, h],
            send_sem=send_sem.at[s, kind], recv_sem=recv_sem.at[s, h],
            device_id={"ctx": target}, device_id_type=MESH,
        )

    def sent(s, kind, first):
        span = glob_ref.at[s, pl.ds(first, HALF)]
        return pltpu.make_async_remote_copy(
            src_ref=span, dst_ref=span,
            send_sem=send_sem.at[s, kind], recv_sem=recv_sem.at[s, 0],
            device_id={"ctx": sibling}, device_id_type=MESH,
        )

    for s in range(NGLOB):
        needs, owner, holds, routes = plans[s]

        @pl.when(owner)
        def _():
            @pl.loop(0, HEADS_HERE)
            def _(h):
                pltpu.make_async_copy(cand_ref.at[h], glob_ref.at[s, h], recv_sem.at[s, h]).start()

        @pl.when(jnp.logical_not(needs))
        def _():
            span = pl.ds(theirs, HALF)
            pltpu.make_async_copy(cand_ref.at[span], glob_ref.at[s, span], fill_sem.at[s, 0]).start()

        @pl.when(jnp.logical_not(holds))
        def _():
            span = pl.ds(mine, HALF)
            pltpu.make_async_copy(cand_ref.at[span], glob_ref.at[s, span], fill_sem.at[s, 1]).start()

    @pl.loop(0, HALF)
    def _(j):
        for s in range(NGLOB):
            needs, owner, holds, routes = plans[s]

            @pl.when(holds)
            def _():
                h = mine + j
                send(s, h, 0, sibling).wait_recv()
                for kind, on, target in routes:

                    @pl.when(on)
                    def _():
                        send(s, h, kind, target).start()

            @pl.when(owner)
            def _():
                h = theirs + j
                send(s, h, 5, sibling).wait_recv()
                send(s, h, 5, sibling).start()

    for s in range(NGLOB):
        needs, owner, holds, routes = plans[s]

        @pl.when(needs & jnp.logical_not(owner))
        def _():
            @pl.loop(0, HALF)
            def _(j):
                send(s, theirs + j, 0, sibling).wait_recv()

        @pl.when(owner)
        def _():
            sent(s, 5, theirs).wait_send()

        for kind, on, target in routes:

            @pl.when(on)
            def _():
                sent(s, kind, mine).wait_send()

        @pl.when(jnp.logical_not(needs))
        def _():
            span = pl.ds(theirs, HALF)
            pltpu.make_async_copy(cand_ref.at[span], glob_ref.at[s, span], fill_sem.at[s, 0]).wait()

        @pl.when(jnp.logical_not(holds))
        def _():
            span = pl.ds(mine, HALF)
            pltpu.make_async_copy(cand_ref.at[span], glob_ref.at[s, span], fill_sem.at[s, 1]).wait()

    @pl.when(me < last)
    def _():
        band_copy().wait_send()

    band_copy().wait_recv()


def exchange(source, kv, cand):
    hbm = pl.BlockSpec(memory_space=pl.ANY)
    return pl.pallas_call(
        functools.partial(exchange_kernel, source),
        out_shape=(
            jax.ShapeDtypeStruct((2, HEADS_HERE, 2, BLK, HS), BF16),
            jax.ShapeDtypeStruct((NGLOB, HEADS_HERE, 2, BLK, HS), BF16),
        ),
        in_specs=[hbm, hbm],
        out_specs=(hbm, hbm),
        scratch_shapes=[
            pltpu.SemaphoreType.DMA((NGLOB, 6)),
            pltpu.SemaphoreType.DMA((NGLOB, HEADS_HERE)),
            pltpu.SemaphoreType.DMA,
            pltpu.SemaphoreType.DMA,
            pltpu.SemaphoreType.DMA((NGLOB, 2)),
        ],
        compiler_params=pltpu.CompilerParams(collective_id=2 + source, has_side_effects=True),
        name=f"exchange_{source}",
    )(kv, cand)


def attention_kernel(
    bias_ref, q_ref, kv_ref, band_ref, glob_ref, gain_ref, out_ref,
    att, square, mine, theirs, send_sem, recv_sem,
):
    h = pl.program_id(0)
    me = lax.axis_index("ctx")
    partner = 1 - lax.axis_index("head")
    barrier = pltpu.get_barrier_semaphore()

    @pl.when(h == 0)
    def _():
        pl.semaphore_signal(barrier, inc=1, device_id={"head": partner}, device_id_type=MESH)
        square[...] = jnp.zeros_like(square)

    edge = jnp.where(me == 0, -jnp.inf, 0.0).astype(F32)
    rows = lax.broadcasted_iota(jnp.int32, (BLK, BLK), 0)
    cols = lax.broadcasted_iota(jnp.int32, (BLK, BLK), 1)
    causal = rows >= cols
    scale = math.log2(math.e) / math.sqrt(HS)
    pieces = []
    for b in range(2):
        q = q_ref[0, b * BLK : (b + 1) * BLK, :]
        if b == 0:
            blocks = [(band_ref.at[0], edge), (band_ref.at[1], edge), (kv_ref.at[0], causal)]
        else:
            blocks = [(band_ref.at[1], edge), (kv_ref.at[0], None), (kv_ref.at[1], causal)]
        blocks += [(glob_ref.at[s], bias_ref[b, s]) for s in range(NGLOB)]
        scores = []
        for ref, mask in blocks:
            one = lax.dot_general(q, ref[0, 0], (((1,), (1,)), ((), ())), preferred_element_type=F32)
            if mask is causal:
                one = jnp.where(causal, one, -jnp.inf)
            elif mask is not None:
                one = one + mask
            scores.append(one)
        top = scores[0]
        for one in scores[1:]:
            top = jnp.maximum(top, one)
        top = jnp.max(top, axis=1, keepdims=True)
        total = None
        blend = None
        for (ref, mask), one in zip(blocks, scores):
            weight = jnp.exp2((one - top) * scale)
            total = weight if total is None else total + weight
            term = jnp.dot(weight.astype(BF16), ref[0, 1], preferred_element_type=F32)
            blend = term if blend is None else blend + term
        total = jnp.sum(total, axis=1, keepdims=True)
        value = blend / total
        att[h, b * BLK : (b + 1) * BLK, :] = value
        pieces.append(value * value)
    square[...] += jnp.concatenate(pieces, 0)

    @pl.when(h == HEADS_HERE - 1)
    def _():
        mine[...] = lax.dot_general(
            jnp.ones((8, HS), F32), square[...], (((1,), (1,)), ((), ())),
            preferred_element_type=F32, precision=lax.Precision.HIGHEST,
        )
        pl.semaphore_wait(barrier, 1)
        copy = pltpu.make_async_remote_copy(
            src_ref=mine, dst_ref=theirs, send_sem=send_sem, recv_sem=recv_sem,
            device_id={"head": partner}, device_id_type=MESH,
        )
        copy.start()
        copy.wait()
        factor = lax.rsqrt((mine[...] + theirs[...]) / D + 1e-06)
        column = jnp.transpose(factor)[:, 0:1]
        for i in range(HEADS_HERE):
            span = slice(i * HS, (i + 1) * HS)
            out_ref[:, span] = (att[i] * gain_ref[:, span] * column).astype(BF16)


def attention(bias, qf, kv, band, glob, gain):
    def per_head(shape, place):
        def index(h):
            return tuple(h if i == place else 0 for i in range(len(shape)))

        return pl.BlockSpec(shape, index)

    whole = HEADS_HERE * HS
    return pl.pallas_call(
        attention_kernel,
        grid=(HEADS_HERE,),
        out_shape=jax.ShapeDtypeStruct((ROWS, whole), BF16),
        in_specs=[
            pl.BlockSpec(memory_space=pltpu.SMEM),
            per_head((1, ROWS, HS), 0),
            per_head((2, 1, 2, BLK, HS), 1),
            per_head((2, 1, 2, BLK, HS), 1),
            per_head((NGLOB, 1, 2, BLK, HS), 1),
            pl.BlockSpec((1, whole), lambda h: (0, 0)),
        ],
        out_specs=pl.BlockSpec((ROWS, whole), lambda h: (0, 0)),
        scratch_shapes=[
            VMEM((HEADS_HERE, ROWS, HS), F32),
            VMEM((ROWS, HS), F32),
            VMEM((8, ROWS), F32),
            VMEM((8, ROWS), F32),
            pltpu.SemaphoreType.DMA,
            pltpu.SemaphoreType.DMA,
        ],
        compiler_params=pltpu.CompilerParams(
            collective_id=1, has_side_effects=True, vmem_limit_bytes=32 * MIB
        ),
        name="attention",
    )(bias, qf, kv, band, glob, gain)


def per_device(q_raw, k_raw, v_raw, g_raw, short_filters, long_filter, out_gain, block_lists):
    phase = block_lists[block_lists.shape[0] - 1, BAND]
    first = lax.axis_index("ctx") * 2
    own = lax.dynamic_slice_in_dim(block_lists, first, 2, 0)[:, BAND:]
    bias = jnp.where(own >= 0, 0.0, -jnp.inf).astype(F32)
    parity = jnp.reshape(phase % 2, (1,))
    qf, kv, cand = features(parity, q_raw, k_raw, v_raw, g_raw, short_filters, long_filter)
    band, glob = lax.switch(
        phase // 2, [functools.partial(exchange, source) for source in range(31)], kv, cand
    )
    return attention(bias, qf, kv, band, glob, out_gain[None, :])


def solution(mesh):
    placed = (
        P("ctx", "head"),
        P("ctx", "head"),
        P("ctx", "head"),
        P("ctx", "head"),
        P(None, None, "head"),
        P(None, "head"),
        P("head"),
        P(),
    )
    return jax.shard_map(
        per_device, mesh=mesh, in_specs=placed, out_specs=P("ctx", "head"), check_vma=False
    )
```

```python
import functools
import math

import jax
import jax.numpy as jnp
from jax import lax
from jax.experimental import pallas as pl
from jax.experimental.pallas import tpu as pltpu
from jax.sharding import PartitionSpec as P

D = 4096
HS = 128
BLK = 128
BAND = 3
NGLOB = 4
TAPS = 3
TAPS_LONG = 7
ROWS = 256
HEADS_HERE = 16
HALF = 8
HALO = 16
LAG = 3
WIDE = 512
COLUMNS = 4
GROUP = 1
PART = 64
MESH = pl.DeviceIdType.MESH
F32 = jnp.float32
BF16 = jnp.bfloat16
VMEM = pltpu.VMEM
MIB = 1024 * 1024


def taps_of(ext, weights, count):
    total = weights[0:1] * ext
    for s in range(1, count):
        total = total + weights[s : s + 1] * pltpu.roll(ext, s, 0)
    return total


def features_kernel(
    parity_ref, q_ref, k_ref, v_ref, g_ref, sf_in, lf_in,
    qf_ref, kv_ref, cand_ref, halo, held, sf_ref, lf_ref, send_sem, recv_sem, load_sem, tap_sem,
):
    me = lax.axis_index("ctx")
    last = lax.axis_size("ctx") - 1
    streams = (q_ref, k_ref, v_ref, g_ref)
    barrier = pltpu.get_barrier_semaphore()

    for other in ((me + last) % (last + 1), (me + 1) % (last + 1)):
        pl.semaphore_signal(barrier, inc=1, device_id={"ctx": other}, device_id_type=MESH)

    def load(i, c):
        span = pl.ds(pl.multiple_of(c * WIDE, WIDE), WIDE)
        return pltpu.make_async_copy(
            streams[i].at[:, span], held.at[i, :, span], load_sem.at[i, c]
        )

    taps = [
        pltpu.make_async_copy(sf_in, sf_ref, tap_sem.at[0]),
        pltpu.make_async_copy(lf_in, lf_ref, tap_sem.at[1]),
    ]
    for copy in taps:
        copy.start()
    for c in range(COLUMNS):
        for i in range(4):
            load(i, c).start()
    pl.semaphore_wait(barrier, 2)

    def tail_copy(i):
        return pltpu.make_async_remote_copy(
            src_ref=streams[i].at[pl.ds(ROWS - HALO, HALO)],
            dst_ref=halo.at[i],
            send_sem=send_sem.at[i],
            recv_sem=recv_sem.at[i],
            device_id={"ctx": me + 1},
            device_id_type=MESH,
        )

    @pl.when(me < last)
    def _():
        for i in range(4):
            tail_copy(i).start()

    @pl.when(me == 0)
    def _():
        halo[...] = jnp.zeros_like(halo)

    def part(h, r):
        cols = pl.ds(pl.multiple_of(h * HS, HS), HS)

        def extended(i):
            if r == 0:
                before = halo[i, :, cols].astype(F32)
                return jnp.concatenate([before, held[i, 0:PART, cols].astype(F32)], 0)
            return held[i, r * PART - HALO : (r + 1) * PART, cols].astype(F32)

        feats = [taps_of(extended(i), sf_ref[:, i, cols], TAPS) for i in range(4)]
        values = taps_of(feats[3] * feats[2], lf_ref[:, cols], TAPS_LONG)
        qf_ref[h, r * PART : (r + 1) * PART, :] = feats[0][HALO:].astype(BF16)
        low = r * PART % BLK
        kv_ref[r * PART // BLK, h, 0, low : low + PART, :] = feats[1][HALO:].astype(BF16)
        kv_ref[r * PART // BLK, h, 1, low : low + PART, :] = values[HALO:].astype(BF16)

    for copy in taps:
        copy.wait()

    @pl.loop(0, COLUMNS)
    def _(c):
        for i in range(4):
            load(i, c).wait()

        @pl.loop(0, HEADS_HERE // COLUMNS)
        def _(n):
            for r in range(1, ROWS // PART):
                part(c * (HEADS_HERE // COLUMNS) + n, r)

    @pl.when(me > 0)
    def _():
        for i in range(4):
            tail_copy(i).wait_recv()

    parity = parity_ref[0]

    @pl.loop(0, HEADS_HERE)
    def _(h):
        part(h, 0)
        cand_ref[h] = kv_ref[parity, h]

    @pl.when(me < last)
    def _():
        for i in range(4):
            tail_copy(i).wait_send()


def features(parity, q_raw, k_raw, v_raw, g_raw, short_filters, long_filter):
    vm = pl.BlockSpec(memory_space=VMEM)
    return pl.pallas_call(
        features_kernel,
        out_shape=(
            jax.ShapeDtypeStruct((HEADS_HERE, ROWS, HS), BF16),
            jax.ShapeDtypeStruct((2, HEADS_HERE, 2, BLK, HS), BF16),
            jax.ShapeDtypeStruct((HEADS_HERE, 2, BLK, HS), BF16),
        ),
        in_specs=[pl.BlockSpec(memory_space=pltpu.SMEM)] + [pl.BlockSpec(memory_space=pl.ANY)] * 6,
        out_specs=(vm, vm, vm),
        scratch_shapes=[
            VMEM((4, HALO, HEADS_HERE * HS), BF16),
            VMEM((4, ROWS, HEADS_HERE * HS), BF16),
            VMEM((TAPS, 4, HEADS_HERE * HS), F32),
            VMEM((TAPS_LONG, HEADS_HERE * HS), F32),
            pltpu.SemaphoreType.DMA((4,)),
            pltpu.SemaphoreType.DMA((4,)),
            pltpu.SemaphoreType.DMA((4, COLUMNS)),
            pltpu.SemaphoreType.DMA((2,)),
        ],
        compiler_params=pltpu.CompilerParams(
            collective_id=0, has_side_effects=True, vmem_limit_bytes=56 * MIB
        ),
        name="features",
    )(parity, q_raw, k_raw, v_raw, g_raw, short_filters, long_filter)


def exchange_kernel(source, kv_ref, cand_ref, band_ref, glob_ref, send_sem, recv_sem, band_send, band_recv, fill_sem):
    x0, z0, c0 = source // 16, source // 2 % 8, source % 2
    me = lax.axis_index("ctx")
    last = lax.axis_size("ctx") - 1
    core = me % 2
    z = me // 2 % 8
    x = me // 16 % 2
    y = me // 32
    steps = (z0 - z + 8) % 8

    def at(yy, xx, zz, cc):
        return ((yy * 2 + xx) * 8 + zz) * 2 + cc

    x_other = at(y, 1 - x, z, core)
    y_up, y_down = at((y + 1) % 4, x, z, core), at((y + 3) % 4, x, z, core)
    sibling = at(y, x, z, 1 - core)
    outer = (me + last + 2 * core) % (last + 1)

    barrier = pltpu.get_barrier_semaphore()
    z_targets = {kind: at(y, x, (z + move) % 8, core) for kind, move in [(6, 7), (7, 1), (8, 5), (9, 2)]}
    z_others = [at(y, x, (z + move) % 8, core) for move in (1, 7, 3, 5, 2, 6)]
    for other in z_others + [x_other, y_up, y_down, sibling, outer]:
        pl.semaphore_signal(barrier, inc=1, device_id={"ctx": other}, device_id_type=MESH)
    pl.semaphore_wait(barrier, 11)

    def band_copy():
        return pltpu.make_async_remote_copy(
            src_ref=kv_ref, dst_ref=band_ref, send_sem=band_send, recv_sem=band_recv,
            device_id={"ctx": me + 1}, device_id_type=MESH,
        )

    @pl.when(me < last)
    def _():
        band_copy().start()

    @pl.when(me == 0)
    def _():
        for b in range(2):
            pltpu.make_async_copy(cand_ref, band_ref.at[b], band_recv).start()

    main = x == (x0 + core) % 2
    at_source = (x == x0) & (steps == 0)
    mine, theirs = core * HALF, (1 - core) * HALF

    plans = []
    for s in range(NGLOB):
        plane = y == s
        along = plane & main
        z_routes = [
            (8, along & (steps == 0), z_targets[8]),
            (9, along & (steps == 0), z_targets[9]),
            (6, along & ((steps == 0) | (steps == 1) | (steps == 3) | (steps == 6)), z_targets[6]),
            (7, along & (steps == 6), z_targets[7]),
        ]
        over_x = plane & (
            (main & jnp.logical_not((core == 1) & (steps == 0)))
            | (jnp.logical_not(main) & (core == 1) & (steps == 0))
        )
        never = y < 0
        up = [
            (y == 0) | ((y == 1) & (core == 0)),
            (y == 1) | ((y == 2) & (core == 0)),
            y == 2,
            never,
        ][s]
        down = [
            (y == 0) | ((y == 3) & (core == 1)),
            ((y == 1) | (y == 0)) & (core == 1),
            never,
            never,
        ][s]
        needs = y >= s
        owner = plane & at_source & (core == c0)
        near_owner = plane & at_source & (core != c0)
        holds = needs if s != 1 else (needs | ((y == 0) & (core == 1)))
        share = needs & jnp.logical_not(near_owner)
        routes = []
        if s < 3:
            routes += [(2, up, y_up)]
        if s < 2:
            routes += [(3, down, y_down)]
        routes = z_routes + [(1, over_x, x_other)] + routes + [(4, share, sibling)]
        depth = [
            jnp.where(y == 0, 0, jnp.where(y == 2, 2, 1)),
            jnp.where(y == 1, 0, jnp.where(y == 3, 2, 1)),
            jnp.where(y == 2, 0, 1),
            0,
        ][s]
        plans.append((needs, owner, holds, routes, depth * LAG))

    def send(s, h, kind, target):
        return pltpu.make_async_remote_copy(
            src_ref=glob_ref.at[s, pl.ds(h, GROUP)], dst_ref=glob_ref.at[s, pl.ds(h, GROUP)],
            send_sem=send_sem.at[s, kind], recv_sem=recv_sem.at[s, h],
            device_id={"ctx": target}, device_id_type=MESH,
        )

    def sent(s, kind, first):
        span = glob_ref.at[s, pl.ds(first, HALF)]
        return pltpu.make_async_remote_copy(
            src_ref=span, dst_ref=span,
            send_sem=send_sem.at[s, kind], recv_sem=recv_sem.at[s, 0],
            device_id={"ctx": sibling}, device_id_type=MESH,
        )

    for s in range(NGLOB):
        needs, owner, holds, routes, lag = plans[s]

        @pl.when(owner)
        def _():
            @pl.loop(0, HEADS_HERE // GROUP)
            def _(i):
                span = pl.ds(i * GROUP, GROUP)
                pltpu.make_async_copy(
                    cand_ref.at[span], glob_ref.at[s, span], recv_sem.at[s, i * GROUP]
                ).start()

        @pl.when(jnp.logical_not(needs))
        def _():
            span = pl.ds(theirs, HALF)
            pltpu.make_async_copy(cand_ref.at[span], glob_ref.at[s, span], fill_sem.at[s, 0]).start()

        @pl.when(jnp.logical_not(holds))
        def _():
            span = pl.ds(mine, HALF)
            pltpu.make_async_copy(cand_ref.at[span], glob_ref.at[s, span], fill_sem.at[s, 1]).start()

    @pl.loop(0, HALF // GROUP + 2 * LAG)
    def _(t):
        for s in (3, 2, 1, 0):
            needs, owner, holds, routes, lag = plans[s]
            j = t - lag
            turn = (j >= 0) & (j < HALF // GROUP)

            @pl.when(holds & turn)
            def _():
                h = mine + j * GROUP
                send(s, h, 0, sibling).wait_recv()
                for kind, on, target in routes:

                    @pl.when(on)
                    def _():
                        send(s, h, kind, target).start()

            @pl.when(owner & turn)
            def _():
                h = theirs + j * GROUP
                send(s, h, 5, sibling).wait_recv()
                send(s, h, 5, sibling).start()

    for s in range(NGLOB):
        needs, owner, holds, routes, lag = plans[s]

        @pl.when(needs & jnp.logical_not(owner))
        def _():
            @pl.loop(0, HALF // GROUP)
            def _(j):
                send(s, theirs + j * GROUP, 0, sibling).wait_recv()

        @pl.when(owner)
        def _():
            sent(s, 5, theirs).wait_send()

        for kind, on, target in routes:

            @pl.when(on)
            def _():
                sent(s, kind, mine).wait_send()

        @pl.when(jnp.logical_not(needs))
        def _():
            span = pl.ds(theirs, HALF)
            pltpu.make_async_copy(cand_ref.at[span], glob_ref.at[s, span], fill_sem.at[s, 0]).wait()

        @pl.when(jnp.logical_not(holds))
        def _():
            span = pl.ds(mine, HALF)
            pltpu.make_async_copy(cand_ref.at[span], glob_ref.at[s, span], fill_sem.at[s, 1]).wait()

    @pl.when(me < last)
    def _():
        band_copy().wait_send()

    band_copy().wait_recv()


def exchange(source, kv, cand):
    vm = pl.BlockSpec(memory_space=VMEM)
    return pl.pallas_call(
        functools.partial(exchange_kernel, source),
        out_shape=(
            jax.ShapeDtypeStruct((2, HEADS_HERE, 2, BLK, HS), BF16),
            jax.ShapeDtypeStruct((NGLOB, HEADS_HERE, 2, BLK, HS), BF16),
        ),
        in_specs=[vm, vm],
        out_specs=(vm, vm),
        scratch_shapes=[
            pltpu.SemaphoreType.DMA((NGLOB, 10)),
            pltpu.SemaphoreType.DMA((NGLOB, HEADS_HERE)),
            pltpu.SemaphoreType.DMA,
            pltpu.SemaphoreType.DMA,
            pltpu.SemaphoreType.DMA((NGLOB, 2)),
        ],
        compiler_params=pltpu.CompilerParams(
            collective_id=2 + source, has_side_effects=True, vmem_limit_bytes=32 * MIB
        ),
        name=f"exchange_{source}",
    )(kv, cand)


def attention_kernel(
    bias_ref, q_ref, kv_ref, band_ref, glob_ref, gain_ref, out_ref,
    att, square, mine, theirs, send_sem, recv_sem,
):
    me = lax.axis_index("ctx")
    partner = 1 - lax.axis_index("head")
    barrier = pltpu.get_barrier_semaphore()

    pl.semaphore_signal(barrier, inc=1, device_id={"head": partner}, device_id_type=MESH)
    square[...] = jnp.zeros_like(square)

    edge = jnp.where(me == 0, -jnp.inf, 0.0).astype(F32)
    rows = lax.broadcasted_iota(jnp.int32, (BLK, BLK), 0)
    cols = lax.broadcasted_iota(jnp.int32, (BLK, BLK), 1)
    causal = jnp.where(rows >= cols, 0.0, -jnp.inf).astype(F32)
    scale = math.log2(math.e) / math.sqrt(HS)

    def times(a, b):
        return lax.dot_general(a, b, (((1,), (1,)), ((), ())), preferred_element_type=F32)

    def mix(a, b):
        return jnp.dot(a.astype(BF16), b, preferred_element_type=F32)

    @pl.loop(0, HEADS_HERE)
    def _(i):
        q = q_ref[i]
        halves = [q[:BLK], q[BLK:]]
        wide = times(q, glob_ref[:, i, 0].reshape(NGLOB * BLK, HS))
        near = times(q, band_ref[1, i, 0])
        first = times(q, kv_ref[0, i, 0])
        extra = [times(halves[0], band_ref[0, i, 0]), times(halves[1], kv_ref[1, i, 0])]
        w_wide, w_near, w_first, w_extra, totals = [], [], [], [], []
        for b in range(2):
            span = slice(b * BLK, (b + 1) * BLK)
            scores = [
                near[span] + edge,
                first[span] + causal if b == 0 else first[span],
                extra[b] + (edge if b == 0 else causal),
            ]
            scores += [
                wide[span, s * BLK : (s + 1) * BLK] + bias_ref[b, s] for s in range(NGLOB)
            ]
            top = scores[0]
            for one in scores[1:]:
                top = jnp.maximum(top, one)
            top = jnp.max(top, axis=1, keepdims=True) * scale
            weights = [jnp.exp2(one * scale - top) for one in scores]
            total = weights[0]
            for one in weights[1:]:
                total = total + one
            totals.append(jnp.sum(total, axis=1, keepdims=True))
            w_near.append(weights[0])
            w_first.append(weights[1])
            w_extra.append(mix(weights[2], (band_ref if b == 0 else kv_ref)[b, i, 1]))
            w_wide.append(jnp.concatenate(weights[3:], 1))
        blend = mix(jnp.concatenate(w_wide, 0), glob_ref[:, i, 1].reshape(NGLOB * BLK, HS))
        blend = blend + mix(jnp.concatenate(w_near, 0), band_ref[1, i, 1])
        blend = blend + mix(jnp.concatenate(w_first, 0), kv_ref[0, i, 1])
        blend = blend + jnp.concatenate(w_extra, 0)
        value = blend / jnp.concatenate(totals, 0)
        att[i] = value
        square[...] += value * value

    mine[...] = lax.dot_general(
        jnp.ones((8, HS), F32), square[...], (((1,), (1,)), ((), ())),
        preferred_element_type=F32, precision=lax.Precision.HIGHEST,
    )
    pl.semaphore_wait(barrier, 1)
    copy = pltpu.make_async_remote_copy(
        src_ref=mine, dst_ref=theirs, send_sem=send_sem, recv_sem=recv_sem,
        device_id={"head": partner}, device_id_type=MESH,
    )
    copy.start()
    copy.wait()
    factor = lax.rsqrt((mine[...] + theirs[...]) / D + 1e-06)
    square[...] = jnp.broadcast_to(jnp.transpose(factor)[:, 0:1], (ROWS, HS))

    @pl.loop(0, HEADS_HERE)
    def _(i):
        span = pl.ds(pl.multiple_of(i * HS, HS), HS)
        out_ref[:, span] = (att[i] * gain_ref[:, span] * square[...]).astype(BF16)


def attention(bias, qf, kv, band, glob, gain):
    vm = pl.BlockSpec(memory_space=VMEM)
    return pl.pallas_call(
        attention_kernel,
        out_shape=jax.ShapeDtypeStruct((ROWS, HEADS_HERE * HS), BF16),
        in_specs=[pl.BlockSpec(memory_space=pltpu.SMEM)] + [vm] * 5,
        out_specs=vm,
        scratch_shapes=[
            VMEM((HEADS_HERE, ROWS, HS), F32),
            VMEM((ROWS, HS), F32),
            VMEM((8, ROWS), F32),
            VMEM((8, ROWS), F32),
            pltpu.SemaphoreType.DMA,
            pltpu.SemaphoreType.DMA,
        ],
        compiler_params=pltpu.CompilerParams(
            collective_id=1, has_side_effects=True, vmem_limit_bytes=32 * MIB
        ),
        name="attention",
    )(bias, qf, kv, band, glob, gain)


def per_device(q_raw, k_raw, v_raw, g_raw, short_filters, long_filter, out_gain, block_lists):
    phase = block_lists[block_lists.shape[0] - 1, BAND]
    first = lax.axis_index("ctx") * 2
    own = lax.dynamic_slice_in_dim(block_lists, first, 2, 0)[:, BAND:]
    bias = jnp.where(own >= 0, 0.0, -jnp.inf).astype(F32)
    parity = jnp.reshape(phase % 2, (1,))
    qf, kv, cand = features(
        parity, q_raw, k_raw, v_raw, g_raw, jnp.transpose(short_filters, (1, 0, 2)), long_filter
    )
    band, glob = lax.switch(
        phase // 2, [functools.partial(exchange, source) for source in range(31)], kv, cand
    )
    return attention(bias, qf, kv, band, glob, out_gain[None, :])


def solution(mesh):
    placed = (
        P("ctx", "head"),
        P("ctx", "head"),
        P("ctx", "head"),
        P("ctx", "head"),
        P(None, None, "head"),
        P(None, "head"),
        P("head"),
        P(),
    )
    return jax.shard_map(
        per_device, mesh=mesh, in_specs=placed, out_specs=P("ctx", "head"), check_vma=False
    )
```

```python
import functools
import math

import jax
import jax.numpy as jnp
from jax import lax
from jax.experimental import pallas as pl
from jax.experimental.pallas import tpu as pltpu
from jax.sharding import PartitionSpec as P

D = 4096
HS = 128
BLK = 128
BAND = 3
NGLOB = 4
TAPS = 3
TAPS_LONG = 7
ROWS = 256
HEADS_HERE = 16
HALF = 8
HALO = 16
LAG = 3
EARLY = 12
BATCH = 4
WIDE = 512
COLUMNS = 4
GROUP = 1
PART = 64
MESH = pl.DeviceIdType.MESH
F32 = jnp.float32
BF16 = jnp.bfloat16
VMEM = pltpu.VMEM
MIB = 1024 * 1024


def taps_of(ext, weights, count):
    total = weights[0:1] * ext
    for s in range(1, count):
        total = total + weights[s : s + 1] * pltpu.roll(ext, s, 0)
    return total


def features_kernel(
    parity_ref, q_ref, k_ref, v_ref, g_ref, sf_in, lf_in,
    qf_ref, kv_ref, cand_ref, halo, held, sf_ref, lf_ref, send_sem, recv_sem, load_sem, tap_sem,
):
    me = lax.axis_index("ctx")
    last = lax.axis_size("ctx") - 1
    streams = (q_ref, k_ref, v_ref, g_ref)
    barrier = pltpu.get_barrier_semaphore()

    for other in ((me + last) % (last + 1), (me + 1) % (last + 1)):
        pl.semaphore_signal(barrier, inc=1, device_id={"ctx": other}, device_id_type=MESH)

    def load(i, c):
        span = pl.ds(pl.multiple_of(c * WIDE, WIDE), WIDE)
        return pltpu.make_async_copy(
            streams[i].at[:, span], held.at[i, :, span], load_sem.at[i, c]
        )

    taps = [
        pltpu.make_async_copy(sf_in, sf_ref, tap_sem.at[0]),
        pltpu.make_async_copy(lf_in, lf_ref, tap_sem.at[1]),
    ]
    for copy in taps:
        copy.start()
    for c in range(COLUMNS):
        for i in range(4):
            load(i, c).start()
    pl.semaphore_wait(barrier, 2)

    def tail_copy(i):
        return pltpu.make_async_remote_copy(
            src_ref=streams[i].at[pl.ds(ROWS - HALO, HALO)],
            dst_ref=halo.at[i],
            send_sem=send_sem.at[i],
            recv_sem=recv_sem.at[i],
            device_id={"ctx": me + 1},
            device_id_type=MESH,
        )

    @pl.when(me < last)
    def _():
        for i in range(4):
            tail_copy(i).start()

    @pl.when(me == 0)
    def _():
        halo[...] = jnp.zeros_like(halo)

    def part(h, r):
        cols = pl.ds(pl.multiple_of(h * HS, HS), HS)

        def extended(i):
            if r == 0:
                before = halo[i, :, cols].astype(F32)
                return jnp.concatenate([before, held[i, 0:PART, cols].astype(F32)], 0)
            return held[i, r * PART - HALO : (r + 1) * PART, cols].astype(F32)

        feats = [taps_of(extended(i), sf_ref[:, i, cols], TAPS) for i in range(4)]
        values = taps_of(feats[3] * feats[2], lf_ref[:, cols], TAPS_LONG)
        qf_ref[h, r * PART : (r + 1) * PART, :] = feats[0][HALO:].astype(BF16)
        low = r * PART % BLK
        kv_ref[r * PART // BLK, h, 0, low : low + PART, :] = feats[1][HALO:].astype(BF16)
        kv_ref[r * PART // BLK, h, 1, low : low + PART, :] = values[HALO:].astype(BF16)

    for copy in taps:
        copy.wait()

    @pl.loop(0, COLUMNS)
    def _(c):
        for i in range(4):
            load(i, c).wait()

        @pl.loop(0, HEADS_HERE // COLUMNS)
        def _(n):
            for r in range(1, ROWS // PART):
                part(c * (HEADS_HERE // COLUMNS) + n, r)

    @pl.when(me > 0)
    def _():
        for i in range(4):
            tail_copy(i).wait_recv()

    parity = parity_ref[0]

    @pl.loop(0, HEADS_HERE)
    def _(h):
        part(h, 0)
        cand_ref[h] = kv_ref[parity, h]

    @pl.when(me < last)
    def _():
        for i in range(4):
            tail_copy(i).wait_send()


def features(parity, q_raw, k_raw, v_raw, g_raw, short_filters, long_filter):
    vm = pl.BlockSpec(memory_space=VMEM)
    return pl.pallas_call(
        features_kernel,
        out_shape=(
            jax.ShapeDtypeStruct((HEADS_HERE, ROWS, HS), BF16),
            jax.ShapeDtypeStruct((2, HEADS_HERE, 2, BLK, HS), BF16),
            jax.ShapeDtypeStruct((HEADS_HERE, 2, BLK, HS), BF16),
        ),
        in_specs=[pl.BlockSpec(memory_space=pltpu.SMEM)] + [pl.BlockSpec(memory_space=pl.ANY)] * 6,
        out_specs=(vm, vm, vm),
        scratch_shapes=[
            VMEM((4, HALO, HEADS_HERE * HS), BF16),
            VMEM((4, ROWS, HEADS_HERE * HS), BF16),
            VMEM((TAPS, 4, HEADS_HERE * HS), F32),
            VMEM((TAPS_LONG, HEADS_HERE * HS), F32),
            pltpu.SemaphoreType.DMA((4,)),
            pltpu.SemaphoreType.DMA((4,)),
            pltpu.SemaphoreType.DMA((4, COLUMNS)),
            pltpu.SemaphoreType.DMA((2,)),
        ],
        compiler_params=pltpu.CompilerParams(
            collective_id=0, has_side_effects=True, vmem_limit_bytes=56 * MIB
        ),
        name="features",
    )(parity, q_raw, k_raw, v_raw, g_raw, short_filters, long_filter)


def exchange_kernel(source, kv_ref, cand_ref, band_ref, glob_ref, send_sem, recv_sem, band_send, band_recv, fill_sem):
    x0, z0, c0 = source // 16, source // 2 % 8, source % 2
    me = lax.axis_index("ctx")
    last = lax.axis_size("ctx") - 1
    core = me % 2
    z = me // 2 % 8
    x = me // 16 % 2
    y = me // 32
    steps = (z0 - z + 8) % 8

    def at(yy, xx, zz, cc):
        return ((yy * 2 + xx) * 8 + zz) * 2 + cc

    x_other = at(y, 1 - x, z, core)
    y_up, y_down = at((y + 1) % 4, x, z, core), at((y + 3) % 4, x, z, core)
    sibling = at(y, x, z, 1 - core)
    outer = (me + last + 2 * core) % (last + 1)

    barrier = pltpu.get_barrier_semaphore()
    z_targets = {kind: at(y, x, (z + move) % 8, core) for kind, move in [(6, 7), (7, 1), (8, 5), (9, 2)]}
    z_others = [at(y, x, (z + move) % 8, core) for move in (1, 7, 3, 5, 2, 6)]
    for other in z_others + [x_other, y_up, y_down, sibling, outer]:
        pl.semaphore_signal(barrier, inc=1, device_id={"ctx": other}, device_id_type=MESH)
    pl.semaphore_wait(barrier, 11)

    def band_copy(b):
        return pltpu.make_async_remote_copy(
            src_ref=kv_ref.at[b, pl.ds(0, EARLY)], dst_ref=band_ref.at[b],
            send_sem=band_send.at[b], recv_sem=band_recv.at[b],
            device_id={"ctx": me + 1}, device_id_type=MESH,
        )

    @pl.when(me < last)
    def _():
        for b in range(2):
            band_copy(b).start()

    @pl.when(me == 0)
    def _():
        for b in range(2):
            pltpu.make_async_copy(
                cand_ref.at[pl.ds(0, EARLY)], band_ref.at[b], band_recv.at[b]
            ).start()

    main = x == (x0 + core) % 2
    at_source = (x == x0) & (steps == 0)
    mine, theirs = core * HALF, (1 - core) * HALF

    plans = []
    for s in range(NGLOB):
        plane = y == s
        along = plane & main
        z_routes = [
            (8, along & (steps == 0), z_targets[8]),
            (9, along & (steps == 0), z_targets[9]),
            (6, along & ((steps == 0) | (steps == 1) | (steps == 3) | (steps == 6)), z_targets[6]),
            (7, along & (steps == 6), z_targets[7]),
        ]
        over_x = plane & (
            (main & jnp.logical_not((core == 1) & (steps == 0)))
            | (jnp.logical_not(main) & (core == 1) & (steps == 0))
        )
        never = y < 0
        up = [
            (y == 0) | ((y == 1) & (core == 0)),
            (y == 1) | ((y == 2) & (core == 0)),
            y == 2,
            never,
        ][s]
        down = [
            (y == 0) | ((y == 3) & (core == 1)),
            ((y == 1) | (y == 0)) & (core == 1),
            never,
            never,
        ][s]
        needs = y >= s
        owner = plane & at_source & (core == c0)
        near_owner = plane & at_source & (core != c0)
        holds = needs if s != 1 else (needs | ((y == 0) & (core == 1)))
        share = needs & jnp.logical_not(near_owner)
        routes = []
        if s < 3:
            routes += [(2, up, y_up)]
        if s < 2:
            routes += [(3, down, y_down)]
        routes = z_routes + [(1, over_x, x_other)] + routes + [(4, share, sibling)]
        depth = [
            jnp.where(y == 0, 0, jnp.where(y == 2, 2, 1)),
            jnp.where(y == 1, 0, jnp.where(y == 3, 2, 1)),
            jnp.where(y == 2, 0, 1),
            0,
        ][s]
        plans.append((needs, owner, holds, routes, depth * LAG))

    def send(s, h, kind, target):
        return pltpu.make_async_remote_copy(
            src_ref=glob_ref.at[s, pl.ds(h, GROUP)], dst_ref=glob_ref.at[s, pl.ds(h, GROUP)],
            send_sem=send_sem.at[s, kind], recv_sem=recv_sem.at[s, h],
            device_id={"ctx": target}, device_id_type=MESH,
        )

    def sent(s, kind, first):
        span = glob_ref.at[s, pl.ds(first, HALF)]
        return pltpu.make_async_remote_copy(
            src_ref=span, dst_ref=span,
            send_sem=send_sem.at[s, kind], recv_sem=recv_sem.at[s, 0],
            device_id={"ctx": sibling}, device_id_type=MESH,
        )

    for s in range(NGLOB):
        needs, owner, holds, routes, lag = plans[s]

        @pl.when(owner)
        def _():
            @pl.loop(0, HEADS_HERE // GROUP)
            def _(i):
                span = pl.ds(i * GROUP, GROUP)
                pltpu.make_async_copy(
                    cand_ref.at[span], glob_ref.at[s, span], recv_sem.at[s, i * GROUP]
                ).start()

        @pl.when(jnp.logical_not(needs))
        def _():
            span = pl.ds(theirs, HALF)
            pltpu.make_async_copy(cand_ref.at[span], glob_ref.at[s, span], fill_sem.at[s, 0]).start()

        @pl.when(jnp.logical_not(holds))
        def _():
            span = pl.ds(mine, HALF)
            pltpu.make_async_copy(cand_ref.at[span], glob_ref.at[s, span], fill_sem.at[s, 1]).start()

    @pl.loop(0, HALF // GROUP + 2 * LAG)
    def _(t):
        for s in (3, 2, 1, 0):
            needs, owner, holds, routes, lag = plans[s]
            j = t - lag
            turn = (j >= 0) & (j < HALF // GROUP)

            @pl.when(holds & turn)
            def _():
                h = mine + j * GROUP
                send(s, h, 0, sibling).wait_recv()
                for kind, on, target in routes:

                    @pl.when(on)
                    def _():
                        send(s, h, kind, target).start()

            @pl.when(owner & turn)
            def _():
                h = theirs + j * GROUP
                send(s, h, 5, sibling).wait_recv()
                send(s, h, 5, sibling).start()

    for s in range(NGLOB):
        needs, owner, holds, routes, lag = plans[s]

        @pl.when(needs & jnp.logical_not(owner))
        def _():
            @pl.loop(0, HALF // GROUP)
            def _(j):
                send(s, theirs + j * GROUP, 0, sibling).wait_recv()

        @pl.when(owner)
        def _():
            sent(s, 5, theirs).wait_send()

        for kind, on, target in routes:

            @pl.when(on)
            def _():
                sent(s, kind, mine).wait_send()

        @pl.when(jnp.logical_not(needs))
        def _():
            span = pl.ds(theirs, HALF)
            pltpu.make_async_copy(cand_ref.at[span], glob_ref.at[s, span], fill_sem.at[s, 0]).wait()

        @pl.when(jnp.logical_not(holds))
        def _():
            span = pl.ds(mine, HALF)
            pltpu.make_async_copy(cand_ref.at[span], glob_ref.at[s, span], fill_sem.at[s, 1]).wait()

    @pl.when(me < last)
    def _():
        for b in range(2):
            band_copy(b).wait_send()

    for b in range(2):
        band_copy(b).wait_recv()


def exchange(source, kv, cand):
    vm = pl.BlockSpec(memory_space=VMEM)
    hbm = pl.BlockSpec(memory_space=pl.ANY)
    return pl.pallas_call(
        functools.partial(exchange_kernel, source),
        out_shape=(
            jax.ShapeDtypeStruct((2, EARLY, 2, BLK, HS), BF16),
            jax.ShapeDtypeStruct((NGLOB, HEADS_HERE, 2, BLK, HS), BF16),
        ),
        in_specs=[vm, vm],
        out_specs=(hbm, hbm),
        scratch_shapes=[
            pltpu.SemaphoreType.DMA((NGLOB, 10)),
            pltpu.SemaphoreType.DMA((NGLOB, HEADS_HERE)),
            pltpu.SemaphoreType.DMA((2,)),
            pltpu.SemaphoreType.DMA((2,)),
            pltpu.SemaphoreType.DMA((NGLOB, 2)),
        ],
        compiler_params=pltpu.CompilerParams(
            collective_id=2 + source, has_side_effects=True, vmem_limit_bytes=32 * MIB
        ),
        name=f"exchange_{source}",
    )(kv, cand)


def attention_kernel(
    bias_ref, q_ref, kv_ref, early_in, glob_in, gain_ref, out_ref,
    att, square, mine, theirs, band_ref, glob_ref,
    send_sem, recv_sem, early_sem, glob_sem, band_send, band_recv,
):
    me = lax.axis_index("ctx")
    last = lax.axis_size("ctx") - 1
    partner = 1 - lax.axis_index("head")
    barrier = pltpu.get_barrier_semaphore()

    pl.semaphore_signal(barrier, inc=1, device_id={"head": partner}, device_id_type=MESH)
    for other in ((me + last) % (last + 1), (me + 1) % (last + 1)):
        pl.semaphore_signal(barrier, inc=1, device_id={"ctx": other}, device_id_type=MESH)

    def early(g):
        span = pl.ds(g * BATCH, BATCH)
        return pltpu.make_async_copy(early_in.at[:, span], band_ref.at[:, span], early_sem.at[g])

    def globals_of(g):
        span = pl.ds(g * BATCH, BATCH)
        return pltpu.make_async_copy(glob_in.at[:, span], glob_ref.at[:, span], glob_sem.at[g])

    def late(b):
        span = pl.ds(EARLY, HEADS_HERE - EARLY)
        return pltpu.make_async_remote_copy(
            src_ref=kv_ref.at[b, span], dst_ref=band_ref.at[b, span],
            send_sem=band_send.at[b], recv_sem=band_recv.at[b],
            device_id={"ctx": me + 1}, device_id_type=MESH,
        )

    for g in range(HEADS_HERE // BATCH):
        globals_of(g).start()
        if g < EARLY // BATCH:
            early(g).start()
    square[...] = jnp.zeros_like(square)

    @pl.when(me == 0)
    def _():
        for b in range(2):
            span = pl.ds(EARLY, HEADS_HERE - EARLY)
            pltpu.make_async_copy(
                kv_ref.at[b, span], band_ref.at[b, span], band_recv.at[b]
            ).start()

    pl.semaphore_wait(barrier, 3)

    @pl.when(me < last)
    def _():
        for b in range(2):
            late(b).start()


    edge = jnp.where(me == 0, -jnp.inf, 0.0).astype(F32)
    rows = lax.broadcasted_iota(jnp.int32, (BLK, BLK), 0)
    cols = lax.broadcasted_iota(jnp.int32, (BLK, BLK), 1)
    causal = jnp.where(rows >= cols, 0.0, -jnp.inf).astype(F32)
    scale = math.log2(math.e) / math.sqrt(HS)

    def times(a, b):
        return lax.dot_general(a, b, (((1,), (1,)), ((), ())), preferred_element_type=F32)

    def mix(a, b):
        return jnp.dot(a.astype(BF16), b, preferred_element_type=F32)

    @pl.loop(0, HEADS_HERE)
    def _(i):
        g = i // BATCH

        @pl.when(i % BATCH == 0)
        def _():
            globals_of(g).wait()

        @pl.when((i % BATCH == 0) & (i < EARLY))
        def _():
            early(g).wait()

        @pl.when(i == EARLY)
        def _():
            for b in range(2):
                late(b).wait_recv()

        q = q_ref[i]
        halves = [q[:BLK], q[BLK:]]
        wide = times(q, glob_ref[:, i, 0].reshape(NGLOB * BLK, HS))
        near = times(q, band_ref[1, i, 0])
        first = times(q, kv_ref[0, i, 0])
        extra = [times(halves[0], band_ref[0, i, 0]), times(halves[1], kv_ref[1, i, 0])]
        w_wide, w_near, w_first, w_extra, totals = [], [], [], [], []
        for b in range(2):
            span = slice(b * BLK, (b + 1) * BLK)
            scores = [
                near[span] + edge,
                first[span] + causal if b == 0 else first[span],
                extra[b] + (edge if b == 0 else causal),
            ]
            scores += [
                wide[span, s * BLK : (s + 1) * BLK] + bias_ref[b, s] for s in range(NGLOB)
            ]
            top = scores[0]
            for one in scores[1:]:
                top = jnp.maximum(top, one)
            top = jnp.max(top, axis=1, keepdims=True) * scale
            weights = [jnp.exp2(one * scale - top) for one in scores]
            total = weights[0]
            for one in weights[1:]:
                total = total + one
            totals.append(1.0 / jnp.sum(total, axis=1, keepdims=True))
            w_near.append(weights[0])
            w_first.append(weights[1])
            w_extra.append(mix(weights[2], (band_ref if b == 0 else kv_ref)[b, i, 1]))
            w_wide.append(jnp.concatenate(weights[3:], 1))
        blend = mix(jnp.concatenate(w_wide, 0), glob_ref[:, i, 1].reshape(NGLOB * BLK, HS))
        blend = blend + mix(jnp.concatenate(w_near, 0), band_ref[1, i, 1])
        blend = blend + mix(jnp.concatenate(w_first, 0), kv_ref[0, i, 1])
        blend = blend + jnp.concatenate(w_extra, 0)
        value = blend * jnp.concatenate(totals, 0)
        att[i] = value
        square[...] += value * value

    mine[...] = jnp.sum(jnp.transpose(square[...]).reshape(HS // 8, 8, ROWS), axis=0)
    copy = pltpu.make_async_remote_copy(
        src_ref=mine, dst_ref=theirs, send_sem=send_sem, recv_sem=recv_sem,
        device_id={"head": partner}, device_id_type=MESH,
    )
    copy.start()
    copy.wait()

    @pl.when(me < last)
    def _():
        for b in range(2):
            late(b).wait_send()

    energy = jnp.sum(mine[...] + theirs[...], axis=0, keepdims=True) / D
    factor = jnp.broadcast_to(lax.rsqrt(energy + 1e-06), (8, ROWS))
    square[...] = jnp.broadcast_to(jnp.transpose(factor)[:, 0:1], (ROWS, HS))

    @pl.loop(0, HEADS_HERE)
    def _(i):
        span = pl.ds(pl.multiple_of(i * HS, HS), HS)
        out_ref[:, span] = (att[i] * gain_ref[:, span] * square[...]).astype(BF16)


def attention(bias, qf, kv, band, glob, gain):
    vm = pl.BlockSpec(memory_space=VMEM)
    hbm = pl.BlockSpec(memory_space=pl.ANY)
    return pl.pallas_call(
        attention_kernel,
        out_shape=jax.ShapeDtypeStruct((ROWS, HEADS_HERE * HS), BF16),
        in_specs=[pl.BlockSpec(memory_space=pltpu.SMEM), vm, vm, hbm, hbm, vm],
        out_specs=vm,
        scratch_shapes=[
            VMEM((HEADS_HERE, ROWS, HS), F32),
            VMEM((ROWS, HS), F32),
            VMEM((8, ROWS), F32),
            VMEM((8, ROWS), F32),
            VMEM((2, HEADS_HERE, 2, BLK, HS), BF16),
            VMEM((NGLOB, HEADS_HERE, 2, BLK, HS), BF16),
            pltpu.SemaphoreType.DMA,
            pltpu.SemaphoreType.DMA,
            pltpu.SemaphoreType.DMA((EARLY // BATCH,)),
            pltpu.SemaphoreType.DMA((HEADS_HERE // BATCH,)),
            pltpu.SemaphoreType.DMA((2,)),
            pltpu.SemaphoreType.DMA((2,)),
        ],
        compiler_params=pltpu.CompilerParams(
            collective_id=1, has_side_effects=True, vmem_limit_bytes=48 * MIB
        ),
        name="attention",
    )(bias, qf, kv, band, glob, gain)


def per_device(q_raw, k_raw, v_raw, g_raw, short_filters, long_filter, out_gain, block_lists):
    phase = block_lists[block_lists.shape[0] - 1, BAND]
    first = lax.axis_index("ctx") * 2
    own = lax.dynamic_slice_in_dim(block_lists, first, 2, 0)[:, BAND:]
    bias = jnp.where(own >= 0, 0.0, -jnp.inf).astype(F32)
    parity = jnp.reshape(phase & 1, (1,))
    qf, kv, cand = features(
        parity, q_raw, k_raw, v_raw, g_raw, jnp.transpose(short_filters, (1, 0, 2)), long_filter
    )
    band, glob = lax.switch(
        lax.shift_right_logical(phase, 1), [functools.partial(exchange, source) for source in range(31)], kv, cand
    )
    return attention(bias, qf, kv, band, glob, out_gain[None, :])


def solution(mesh):
    placed = (
        P("ctx", "head"),
        P("ctx", "head"),
        P("ctx", "head"),
        P("ctx", "head"),
        P(None, None, "head"),
        P(None, "head"),
        P("head"),
        P(),
    )
    return jax.shard_map(
        per_device, mesh=mesh, in_specs=placed, out_specs=P("ctx", "head"), check_vma=False
    )
```

```python
import functools
import math

import jax
import jax.numpy as jnp
from jax import lax
from jax.experimental import pallas as pl
from jax.experimental.pallas import tpu as pltpu
from jax.sharding import PartitionSpec as P

D = 4096
HS = 128
BLK = 128
BAND = 3
NGLOB = 4
TAPS = 3
TAPS_LONG = 7
ROWS = 256
HEADS_HERE = 16
HALF = 8
HALO = 16
LAG = 3
EARLY = 12
BATCH = 4
WIDE = 512
COLUMNS = 4
GROUP = 1
PART = 64
MESH = pl.DeviceIdType.MESH
F32 = jnp.float32
BF16 = jnp.bfloat16
VMEM = pltpu.VMEM
MIB = 1024 * 1024


def taps_of(ext, weights, count):
    total = weights[0:1] * ext
    for s in range(1, count):
        total = total + weights[s : s + 1] * pltpu.roll(ext, s, 0)
    return total


def features_kernel(
    parity_ref, q_ref, k_ref, v_ref, g_ref, sf_in, lf_in,
    qf_ref, kv_ref, cand_ref, halo, held, sf_ref, lf_ref, send_sem, recv_sem, load_sem, tap_sem,
):
    me = lax.axis_index("ctx")
    last = lax.axis_size("ctx") - 1
    streams = (q_ref, k_ref, v_ref, g_ref)
    barrier = pltpu.get_barrier_semaphore()

    for other in ((me + last) % (last + 1), (me + 1) % (last + 1)):
        pl.semaphore_signal(barrier, inc=1, device_id={"ctx": other}, device_id_type=MESH)

    def load(i, c):
        span = pl.ds(pl.multiple_of(c * WIDE, WIDE), WIDE)
        return pltpu.make_async_copy(
            streams[i].at[:, span], held.at[i, :, span], load_sem.at[i, c]
        )

    taps = [
        pltpu.make_async_copy(sf_in, sf_ref, tap_sem.at[0]),
        pltpu.make_async_copy(lf_in, lf_ref, tap_sem.at[1]),
    ]
    for copy in taps:
        copy.start()
    for c in range(COLUMNS):
        for i in range(4):
            load(i, c).start()
    pl.semaphore_wait(barrier, 2)

    def tail_copy(i):
        return pltpu.make_async_remote_copy(
            src_ref=streams[i].at[pl.ds(ROWS - HALO, HALO)],
            dst_ref=halo.at[i],
            send_sem=send_sem.at[i],
            recv_sem=recv_sem.at[i],
            device_id={"ctx": me + 1},
            device_id_type=MESH,
        )

    @pl.when(me < last)
    def _():
        for i in range(4):
            tail_copy(i).start()

    @pl.when(me == 0)
    def _():
        halo[...] = jnp.zeros_like(halo)

    def part(h, r):
        cols = pl.ds(pl.multiple_of(h * HS, HS), HS)

        def extended(i):
            if r == 0:
                before = halo[i, :, cols].astype(F32)
                return jnp.concatenate([before, held[i, 0:PART, cols].astype(F32)], 0)
            return held[i, r * PART - HALO : (r + 1) * PART, cols].astype(F32)

        feats = [taps_of(extended(i), sf_ref[:, i, cols], TAPS) for i in range(4)]
        values = taps_of(feats[3] * feats[2], lf_ref[:, cols], TAPS_LONG)
        qf_ref[h, r * PART : (r + 1) * PART, :] = feats[0][HALO:].astype(BF16)
        low = r * PART % BLK
        kv_ref[r * PART // BLK, h, 0, low : low + PART, :] = feats[1][HALO:].astype(BF16)
        kv_ref[r * PART // BLK, h, 1, low : low + PART, :] = values[HALO:].astype(BF16)

    for copy in taps:
        copy.wait()

    @pl.loop(0, COLUMNS)
    def _(c):
        for i in range(4):
            load(i, c).wait()

        @pl.loop(0, HEADS_HERE // COLUMNS)
        def _(n):
            for r in range(1, ROWS // PART):
                part(c * (HEADS_HERE // COLUMNS) + n, r)

    @pl.when(me > 0)
    def _():
        for i in range(4):
            tail_copy(i).wait_recv()

    parity = parity_ref[0]

    @pl.loop(0, HEADS_HERE)
    def _(h):
        part(h, 0)
        cand_ref[h] = kv_ref[parity, h]

    @pl.when(me < last)
    def _():
        for i in range(4):
            tail_copy(i).wait_send()


def features(parity, q_raw, k_raw, v_raw, g_raw, short_filters, long_filter):
    vm = pl.BlockSpec(memory_space=VMEM)
    return pl.pallas_call(
        features_kernel,
        out_shape=(
            jax.ShapeDtypeStruct((HEADS_HERE, ROWS, HS), BF16),
            jax.ShapeDtypeStruct((2, HEADS_HERE, 2, BLK, HS), BF16),
            jax.ShapeDtypeStruct((HEADS_HERE, 2, BLK, HS), BF16),
        ),
        in_specs=[pl.BlockSpec(memory_space=pltpu.SMEM)] + [pl.BlockSpec(memory_space=pl.ANY)] * 6,
        out_specs=(vm, vm, vm),
        scratch_shapes=[
            VMEM((4, HALO, HEADS_HERE * HS), BF16),
            VMEM((4, ROWS, HEADS_HERE * HS), BF16),
            VMEM((TAPS, 4, HEADS_HERE * HS), F32),
            VMEM((TAPS_LONG, HEADS_HERE * HS), F32),
            pltpu.SemaphoreType.DMA((4,)),
            pltpu.SemaphoreType.DMA((4,)),
            pltpu.SemaphoreType.DMA((4, COLUMNS)),
            pltpu.SemaphoreType.DMA((2,)),
        ],
        compiler_params=pltpu.CompilerParams(
            collective_id=0, has_side_effects=True, vmem_limit_bytes=56 * MIB
        ),
        name="features",
    )(parity, q_raw, k_raw, v_raw, g_raw, short_filters, long_filter)


def exchange_kernel(source, kv_ref, cand_ref, band_ref, glob_ref, send_sem, recv_sem, band_send, band_recv, fill_sem):
    x0, z0, c0 = source // 16, source // 2 % 8, source % 2
    me = lax.axis_index("ctx")
    last = lax.axis_size("ctx") - 1
    core = me % 2
    z = me // 2 % 8
    x = me // 16 % 2
    y = me // 32
    steps = (z0 - z + 8) % 8

    def at(yy, xx, zz, cc):
        return ((yy * 2 + xx) * 8 + zz) * 2 + cc

    x_other = at(y, 1 - x, z, core)
    y_up, y_down = at((y + 1) % 4, x, z, core), at((y + 3) % 4, x, z, core)
    sibling = at(y, x, z, 1 - core)
    outer = (me + last + 2 * core) % (last + 1)

    barrier = pltpu.get_barrier_semaphore()
    z_targets = {kind: at(y, x, (z + move) % 8, core) for kind, move in [(0, 7), (2, 5)]}
    z_others = [at(y, x, (z + move) % 8, core) for move in (1, 7, 3, 5)]
    for other in z_others + [x_other, y_up, y_down, sibling, outer]:
        pl.semaphore_signal(barrier, inc=1, device_id={"ctx": other}, device_id_type=MESH)
    pl.semaphore_wait(barrier, 9)

    def band_copy(b):
        return pltpu.make_async_remote_copy(
            src_ref=kv_ref.at[b, pl.ds(0, EARLY)], dst_ref=band_ref.at[b],
            send_sem=band_send.at[b], recv_sem=band_recv.at[b],
            device_id={"ctx": me + 1}, device_id_type=MESH,
        )

    @pl.when(me < last)
    def _():
        for b in range(2):
            band_copy(b).start()

    @pl.when(me == 0)
    def _():
        for b in range(2):
            pltpu.make_async_copy(
                cand_ref.at[pl.ds(0, EARLY)], band_ref.at[b], band_recv.at[b]
            ).start()

    main = x == (x0 + core) % 2
    at_source = (x == x0) & (steps == 0)
    mine, theirs = core * HALF, (1 - core) * HALF

    plans = []
    for s in range(NGLOB):
        plane = y == s
        along = plane & main
        z_routes = [
            (2, along & ((steps == 0) | (steps == 3)), z_targets[2]),
            (0, along & (steps != 2) & (steps != 5) & (steps != 7), z_targets[0]),
        ]
        over_x = plane & (
            (main & jnp.logical_not((core == 1) & (steps == 0)))
            | (jnp.logical_not(main) & (core == 1) & (steps == 0))
        )
        never = y < 0
        up = [
            (y == 0) | ((y == 1) & (core == 0)),
            (y == 1) | ((y == 2) & (core == 0)),
            y == 2,
            never,
        ][s]
        down = [
            (y == 0) | ((y == 3) & (core == 1)),
            ((y == 1) | (y == 0)) & (core == 1),
            never,
            never,
        ][s]
        needs = y >= s
        owner = plane & at_source & (core == c0)
        near_owner = plane & at_source & (core != c0)
        holds = needs if s != 1 else (needs | ((y == 0) & (core == 1)))
        share = needs & jnp.logical_not(near_owner)
        routes = []
        if s < 3:
            routes += [(3, up, y_up)]
        if s < 2:
            routes += [(4, down, y_down)]
        routes = z_routes + [(1, over_x, x_other)] + routes + [(5, share, sibling)]
        depth = [
            jnp.where(y == 0, 0, jnp.where(y == 2, 2, 1)),
            jnp.where(y == 1, 0, jnp.where(y == 3, 2, 1)),
            jnp.where(y == 2, 0, 1),
            0,
        ][s]
        plans.append((needs, owner, holds, routes, depth * LAG))

    def send(s, h, kind, target):
        return pltpu.make_async_remote_copy(
            src_ref=glob_ref.at[s, pl.ds(h, GROUP)], dst_ref=glob_ref.at[s, pl.ds(h, GROUP)],
            send_sem=send_sem.at[s, kind], recv_sem=recv_sem.at[s, h],
            device_id={"ctx": target}, device_id_type=MESH,
        )

    def sent(s, kind, first):
        span = glob_ref.at[s, pl.ds(first, HALF)]
        return pltpu.make_async_remote_copy(
            src_ref=span, dst_ref=span,
            send_sem=send_sem.at[s, kind], recv_sem=recv_sem.at[s, 0],
            device_id={"ctx": sibling}, device_id_type=MESH,
        )

    for s in range(NGLOB):
        needs, owner, holds, routes, lag = plans[s]

        @pl.when(owner)
        def _():
            @pl.loop(0, HEADS_HERE // GROUP)
            def _(i):
                span = pl.ds(i * GROUP, GROUP)
                pltpu.make_async_copy(
                    cand_ref.at[span], glob_ref.at[s, span], recv_sem.at[s, i * GROUP]
                ).start()

        @pl.when(jnp.logical_not(needs))
        def _():
            span = pl.ds(theirs, HALF)
            pltpu.make_async_copy(cand_ref.at[span], glob_ref.at[s, span], fill_sem.at[s, 0]).start()

        @pl.when(jnp.logical_not(holds))
        def _():
            span = pl.ds(mine, HALF)
            pltpu.make_async_copy(cand_ref.at[span], glob_ref.at[s, span], fill_sem.at[s, 1]).start()

    @pl.loop(0, HALF // GROUP + 2 * LAG)
    def _(t):
        for s in (3, 2, 1, 0):
            needs, owner, holds, routes, lag = plans[s]
            j = t - lag
            turn = (j >= 0) & (j < HALF // GROUP)

            @pl.when(holds & turn)
            def _():
                h = mine + j * GROUP
                send(s, h, 0, sibling).wait_recv()
                for kind, on, target in routes:

                    @pl.when(on)
                    def _():
                        send(s, h, kind, target).start()

            @pl.when(owner & turn)
            def _():
                h = theirs + j * GROUP
                send(s, h, 6, sibling).wait_recv()
                send(s, h, 6, sibling).start()

    for s in range(NGLOB):
        needs, owner, holds, routes, lag = plans[s]

        @pl.when(needs & jnp.logical_not(owner))
        def _():
            @pl.loop(0, HALF // GROUP)
            def _(j):
                send(s, theirs + j * GROUP, 0, sibling).wait_recv()

        @pl.when(owner)
        def _():
            sent(s, 6, theirs).wait_send()

        for kind, on, target in routes:

            @pl.when(on)
            def _():
                sent(s, kind, mine).wait_send()

        @pl.when(jnp.logical_not(needs))
        def _():
            span = pl.ds(theirs, HALF)
            pltpu.make_async_copy(cand_ref.at[span], glob_ref.at[s, span], fill_sem.at[s, 0]).wait()

        @pl.when(jnp.logical_not(holds))
        def _():
            span = pl.ds(mine, HALF)
            pltpu.make_async_copy(cand_ref.at[span], glob_ref.at[s, span], fill_sem.at[s, 1]).wait()

    @pl.when(me < last)
    def _():
        for b in range(2):
            band_copy(b).wait_send()

    for b in range(2):
        band_copy(b).wait_recv()


def exchange(source, kv, cand):
    vm = pl.BlockSpec(memory_space=VMEM)
    hbm = pl.BlockSpec(memory_space=pl.ANY)
    return pl.pallas_call(
        functools.partial(exchange_kernel, source),
        out_shape=(
            jax.ShapeDtypeStruct((2, EARLY, 2, BLK, HS), BF16),
            jax.ShapeDtypeStruct((NGLOB, HEADS_HERE, 2, BLK, HS), BF16),
        ),
        in_specs=[vm, vm],
        out_specs=(hbm, hbm),
        scratch_shapes=[
            pltpu.SemaphoreType.DMA((NGLOB, 7)),
            pltpu.SemaphoreType.DMA((NGLOB, HEADS_HERE)),
            pltpu.SemaphoreType.DMA((2,)),
            pltpu.SemaphoreType.DMA((2,)),
            pltpu.SemaphoreType.DMA((NGLOB, 2)),
        ],
        compiler_params=pltpu.CompilerParams(
            collective_id=2 + source, has_side_effects=True, vmem_limit_bytes=32 * MIB
        ),
        name=f"exchange_{source}",
    )(kv, cand)


def attention_kernel(
    bias_ref, q_ref, kv_ref, early_in, glob_in, gain_ref, out_ref,
    att, square, mine, theirs, band_ref, glob_ref,
    send_sem, recv_sem, early_sem, glob_sem, band_send, band_recv,
):
    me = lax.axis_index("ctx")
    last = lax.axis_size("ctx") - 1
    partner = 1 - lax.axis_index("head")
    barrier = pltpu.get_barrier_semaphore()

    pl.semaphore_signal(barrier, inc=1, device_id={"head": partner}, device_id_type=MESH)
    for other in ((me + last) % (last + 1), (me + 1) % (last + 1)):
        pl.semaphore_signal(barrier, inc=1, device_id={"ctx": other}, device_id_type=MESH)

    def early(g):
        span = pl.ds(g * BATCH, BATCH)
        return pltpu.make_async_copy(early_in.at[:, span], band_ref.at[:, span], early_sem.at[g])

    def globals_of(g):
        span = pl.ds(g * BATCH, BATCH)
        return pltpu.make_async_copy(glob_in.at[:, span], glob_ref.at[:, span], glob_sem.at[g])

    def late(b):
        span = pl.ds(EARLY, HEADS_HERE - EARLY)
        return pltpu.make_async_remote_copy(
            src_ref=kv_ref.at[b, span], dst_ref=band_ref.at[b, span],
            send_sem=band_send.at[b], recv_sem=band_recv.at[b],
            device_id={"ctx": me + 1}, device_id_type=MESH,
        )

    for g in range(HEADS_HERE // BATCH):
        globals_of(g).start()
        if g < EARLY // BATCH:
            early(g).start()
    square[...] = jnp.zeros_like(square)

    @pl.when(me == 0)
    def _():
        for b in range(2):
            span = pl.ds(EARLY, HEADS_HERE - EARLY)
            pltpu.make_async_copy(
                kv_ref.at[b, span], band_ref.at[b, span], band_recv.at[b]
            ).start()

    pl.semaphore_wait(barrier, 3)

    @pl.when(me < last)
    def _():
        for b in range(2):
            late(b).start()


    edge = jnp.where(me == 0, -jnp.inf, 0.0).astype(F32)
    rows = lax.broadcasted_iota(jnp.int32, (BLK, BLK), 0)
    cols = lax.broadcasted_iota(jnp.int32, (BLK, BLK), 1)
    causal = jnp.where(rows >= cols, 0.0, -jnp.inf).astype(F32)
    scale = math.log2(math.e) / math.sqrt(HS)

    def times(a, b):
        return lax.dot_general(a, b, (((1,), (1,)), ((), ())), preferred_element_type=F32)

    def mix(a, b):
        return jnp.dot(a.astype(BF16), b, preferred_element_type=F32)

    @pl.loop(0, HEADS_HERE)
    def _(i):
        g = i // BATCH

        @pl.when(i % BATCH == 0)
        def _():
            globals_of(g).wait()

        @pl.when((i % BATCH == 0) & (i < EARLY))
        def _():
            early(g).wait()

        @pl.when(i == EARLY)
        def _():
            for b in range(2):
                late(b).wait_recv()

        q = q_ref[i]
        halves = [q[:BLK], q[BLK:]]
        wide = times(q, glob_ref[:, i, 0].reshape(NGLOB * BLK, HS))
        near = times(q, band_ref[1, i, 0])
        first = times(q, kv_ref[0, i, 0])
        extra = [times(halves[0], band_ref[0, i, 0]), times(halves[1], kv_ref[1, i, 0])]
        w_wide, w_near, w_first, w_extra, totals = [], [], [], [], []
        for b in range(2):
            span = slice(b * BLK, (b + 1) * BLK)
            scores = [
                near[span] + edge,
                first[span] + causal if b == 0 else first[span],
                extra[b] + (edge if b == 0 else causal),
            ]
            scores += [
                wide[span, s * BLK : (s + 1) * BLK] + bias_ref[b, s] for s in range(NGLOB)
            ]
            top = scores[0]
            for one in scores[1:]:
                top = jnp.maximum(top, one)
            top = jnp.max(top, axis=1, keepdims=True) * scale
            weights = [jnp.exp2(one * scale - top) for one in scores]
            total = weights[0]
            for one in weights[1:]:
                total = total + one
            totals.append(1.0 / jnp.sum(total, axis=1, keepdims=True))
            w_near.append(weights[0])
            w_first.append(weights[1])
            w_extra.append(mix(weights[2], (band_ref if b == 0 else kv_ref)[b, i, 1]))
            w_wide.append(jnp.concatenate(weights[3:], 1))
        blend = mix(jnp.concatenate(w_wide, 0), glob_ref[:, i, 1].reshape(NGLOB * BLK, HS))
        blend = blend + mix(jnp.concatenate(w_near, 0), band_ref[1, i, 1])
        blend = blend + mix(jnp.concatenate(w_first, 0), kv_ref[0, i, 1])
        blend = blend + jnp.concatenate(w_extra, 0)
        value = blend * jnp.concatenate(totals, 0)
        att[i] = value
        square[...] += value * value

    mine[...] = jnp.sum(jnp.transpose(square[...]).reshape(HS // 8, 8, ROWS), axis=0)
    copy = pltpu.make_async_remote_copy(
        src_ref=mine, dst_ref=theirs, send_sem=send_sem, recv_sem=recv_sem,
        device_id={"head": partner}, device_id_type=MESH,
    )
    copy.start()
    copy.wait()

    @pl.when(me < last)
    def _():
        for b in range(2):
            late(b).wait_send()

    energy = jnp.sum(mine[...] + theirs[...], axis=0, keepdims=True) / D
    factor = jnp.broadcast_to(lax.rsqrt(energy + 1e-06), (8, ROWS))
    square[...] = jnp.broadcast_to(jnp.transpose(factor)[:, 0:1], (ROWS, HS))

    @pl.loop(0, HEADS_HERE)
    def _(i):
        span = pl.ds(pl.multiple_of(i * HS, HS), HS)
        out_ref[:, span] = (att[i] * gain_ref[:, span] * square[...]).astype(BF16)


def attention(bias, qf, kv, band, glob, gain):
    vm = pl.BlockSpec(memory_space=VMEM)
    hbm = pl.BlockSpec(memory_space=pl.ANY)
    return pl.pallas_call(
        attention_kernel,
        out_shape=jax.ShapeDtypeStruct((ROWS, HEADS_HERE * HS), BF16),
        in_specs=[pl.BlockSpec(memory_space=pltpu.SMEM), vm, vm, hbm, hbm, vm],
        out_specs=vm,
        scratch_shapes=[
            VMEM((HEADS_HERE, ROWS, HS), F32),
            VMEM((ROWS, HS), F32),
            VMEM((8, ROWS), F32),
            VMEM((8, ROWS), F32),
            VMEM((2, HEADS_HERE, 2, BLK, HS), BF16),
            VMEM((NGLOB, HEADS_HERE, 2, BLK, HS), BF16),
            pltpu.SemaphoreType.DMA,
            pltpu.SemaphoreType.DMA,
            pltpu.SemaphoreType.DMA((EARLY // BATCH,)),
            pltpu.SemaphoreType.DMA((HEADS_HERE // BATCH,)),
            pltpu.SemaphoreType.DMA((2,)),
            pltpu.SemaphoreType.DMA((2,)),
        ],
        compiler_params=pltpu.CompilerParams(
            collective_id=1, has_side_effects=True, vmem_limit_bytes=48 * MIB
        ),
        name="attention",
    )(bias, qf, kv, band, glob, gain)


def per_device(q_raw, k_raw, v_raw, g_raw, short_filters, long_filter, out_gain, block_lists):
    phase = block_lists[block_lists.shape[0] - 1, BAND]
    first = lax.axis_index("ctx") * 2
    own = lax.dynamic_slice_in_dim(block_lists, first, 2, 0)[:, BAND:]
    bias = jnp.where(own >= 0, 0.0, -jnp.inf).astype(F32)
    parity = jnp.reshape(phase & 1, (1,))
    qf, kv, cand = features(
        parity, q_raw, k_raw, v_raw, g_raw, jnp.transpose(short_filters, (1, 0, 2)), long_filter
    )
    band, glob = lax.switch(
        lax.shift_right_logical(phase, 1), [functools.partial(exchange, source) for source in range(31)], kv, cand
    )
    return attention(bias, qf, kv, band, glob, out_gain[None, :])


def solution(mesh):
    placed = (
        P("ctx", "head"),
        P("ctx", "head"),
        P("ctx", "head"),
        P("ctx", "head"),
        P(None, None, "head"),
        P(None, "head"),
        P("head"),
        P(),
    )
    return jax.shard_map(
        per_device, mesh=mesh, in_specs=placed, out_specs=P("ctx", "head"), check_vma=False
    )
```
